256 devices in a mesh: row: 16 (over x, y), col: 8 (over z), layer: 2 (over core).
Axes of the slice: x: 4, y: 4, z: 8, core: 2. Of those that a mesh axis runs over, the one named last changes fastest.
Arguments:
- a_blocks: bfloat16 [8, 16, 16, 128, 128], P('col', 'row'), may hold values from -6 to 6
- a_rows: int32 [8, 16, 16], P('col', 'row'), may hold values from 0 to 8, as said below
- a_cols: int32 [8, 16, 16], P('col', 'row'), may hold values from 0 to 3, as said below
- b_blocks: bfloat16 [16, 16, 8, 128, 128], P('col', 'row'), may hold values from -0.09375 to 0.09375
- b_rows: int32 [16, 16, 8], P('col', 'row'), may hold values from 0 to 4, as said below
- b_cols: int32 [16, 16, 8], P('col', 'row'), may hold values from 0 to 3, as said below
- prod_keep: int32 [64, 16, 64], P('col', None, 'row'), may hold values 0 or 1
- res_keep: int32 [64, 64], P('col', ('row', 'layer')), may hold values 0 or 1
Outputs:
- c_blocks: bfloat16 [8192, 8192], P('col', ('row', 'layer'))
The draws below stay inside these ranges and needn't reach their ends.
Inputs may be any that keep to these rules, and one draw needn't show every extreme that they name: `a_rows`: within one tile the live slots name distinct blocks; a row of 8 marks an empty slot, whose column is 0 and whose block is ignored. Every tile has at least one live slot, some tile is full and some tile has empty slots. `a_cols`: column of each slot of A; 0 in empty slots. `b_rows`: within one tile the live slots name distinct blocks; a row of 4 marks an empty slot, whose column is 0 and whose block is ignored. Every tile has at least one live slot, some tile is full and some tile has empty slots. `b_cols`: column of each slot of B; 0 in empty slots.
All inputs are finite; a program needn't handle non-finite values. No bound on the sum of `prod_keep` or of `res_keep` on one device may be relied on, other than what follows from the above.
Results may differ from the reference program's by a relative error of at most 0.001.
Values may be sent and summed in bfloat16 or wider, within the bound.
No kernel may reach another device: no remote copies, remote signals or barrier semaphores. Data moves between devices by JAX's collectives and lax.ppermute only.
A program may use at most 64 MiB of HBM per device.

```python
import jax
import jax.numpy as jnp
from jax import lax

BLK = 128
RB = 8
CB = 4
KP = 4
NK = 16
BANDS = 8
BP = 2
LA = 16
LB = 8
MB = 64
NB = 64


def occupancy(key, tiles, slots, height, width):
    tile_keys = jax.random.split(key, tiles)
    places = jax.vmap(lambda one_key: jax.random.permutation(one_key, height * width)[:slots])(tile_keys)
    fewest = max(1, slots // 4)
    counts = jax.random.randint(jax.random.fold_in(key, 7), (tiles,), fewest, slots + 1)
    counts = counts.at[0].set(slots).at[1].set(fewest)
    live = jnp.arange(slots)[None, :] < counts[:, None]
    rows = jnp.where(live, places // width, height).astype(jnp.int32)
    cols = jnp.where(live, places % width, 0).astype(jnp.int32)
    return (rows, cols)


def draw_a_rows(key, part):
    rows, cols = occupancy(jax.random.fold_in(key, 11), BANDS * NK, LA, RB, KP)
    return rows.reshape(BANDS, NK, LA)


def draw_a_cols(key, part):
    rows, cols = occupancy(jax.random.fold_in(key, 11), BANDS * NK, LA, RB, KP)
    return cols.reshape(BANDS, NK, LA)


def draw_b_rows(key, part):
    rows, cols = occupancy(jax.random.fold_in(key, 12), NK * NK, LB, KP, CB)
    return rows.reshape(NK, NK, LB)


def draw_b_cols(key, part):
    rows, cols = occupancy(jax.random.fold_in(key, 12), NK * NK, LB, KP, CB)
    return cols.reshape(NK, NK, LB)


def with_ends(drawn, key, least, largest):
    place = [jax.random.randint(jax.random.fold_in(key, axis), (), 0, length) for axis, length in enumerate(drawn.shape)]
    longest = drawn.shape.index(max(drawn.shape))
    next_to = place[:longest] + [(place[longest] + 1) % drawn.shape[longest]] + place[longest + 1:]
    return drawn.at[tuple(place)].set(least).at[tuple(next_to)].set(largest)


def block_levels(key, shape, shards, smallest, high):
    loudness = 1.0
    for dim, blocks in shards:
        heights = jax.random.uniform(jax.random.fold_in(jax.random.fold_in(key, 6), dim), (blocks,), jnp.float32, smallest / len(shards), high / len(shards))
        loudness = loudness * jnp.repeat(jnp.exp(heights), shape[dim] // blocks).reshape((-1,) + (1,) * (len(shape) - 1 - dim))
    return loudness


def centred(stream_key, shape, scale, reach, shards=(), kind=jnp.bfloat16):
    level = block_levels(stream_key, shape, shards, -0.22, 0.18) if shards else 1.0
    result = jax.random.normal(stream_key, shape, jnp.float32) * scale * level
    return jnp.minimum(jnp.maximum(result, -reach), reach).astype(kind)


def setup_inputs(seed: int = 0) -> dict:
    key_list = jax.random.split(jax.random.key(seed), 9)
    a_blocks = centred(key_list[0], (BANDS, NK, LA, BLK, BLK), 1.0, 6.0, ((0, 8), (1, 16)))
    a_rows = draw_a_rows(jax.random.fold_in(key_list[8], 71), 0)
    a_cols = draw_a_cols(jax.random.fold_in(key_list[8], 71), 0)
    b_blocks = centred(key_list[3], (NK, NK, LB, BLK, BLK), (NK * KP * BLK // 2) ** -0.5, 0.09375, ((0, 8), (1, 16)))
    b_rows = draw_b_rows(jax.random.fold_in(key_list[8], 71), 0)
    b_cols = draw_b_cols(jax.random.fold_in(key_list[8], 71), 0)
    prod_keep = with_ends((jax.random.randint(key_list[6], (MB, NK, NB), 0, 4) < 3).astype(jnp.int32), jax.random.fold_in(key_list[6], 1), 0, 1)
    res_keep = with_ends((jax.random.randint(key_list[7], (MB, NB), 0, 8) < 7).astype(jnp.int32), jax.random.fold_in(key_list[7], 1), 0, 1)
    return {"a_blocks": a_blocks, "a_rows": a_rows, "a_cols": a_cols, "b_blocks": b_blocks, "b_rows": b_rows, "b_cols": b_cols, "prod_keep": prod_keep, "res_keep": res_keep}


def spread_tiles(blocks, rows, cols, height, width):
    position = rows * width + cols
    targets = jnp.arange(height * width, dtype=jnp.int32)
    picker = (position[:, :, None] == targets[None, None, :]).astype(jnp.float32)
    placed = jnp.einsum("tsp,tsxy->tpxy", picker, blocks.astype(jnp.float32))
    return placed.reshape(blocks.shape[0], height, width, BLK, BLK)


def reference(a_blocks, a_rows, a_cols, b_blocks, b_rows, b_cols, prod_keep, res_keep):
    a_stored = spread_tiles(a_blocks.reshape(BANDS * NK, LA, BLK, BLK), a_rows.reshape(BANDS * NK, LA), a_cols.reshape(BANDS * NK, LA), RB, KP)
    a_stored = a_stored.reshape(BANDS, NK, RB, KP, BLK, BLK)
    band_ids = jnp.arange(BANDS, dtype=jnp.int32)[:, None]
    panel_ids = jnp.arange(NK, dtype=jnp.int32)
    a_order = (panel_ids[None, :] - band_ids * BP) % NK
    a_true = a_stored[band_ids, a_order]
    a_mat = a_true.transpose(0, 1, 2, 4, 3, 5).reshape(BANDS, NK, RB * BLK, KP * BLK).astype(jnp.bfloat16)

    b_stored = spread_tiles(b_blocks.reshape(NK * NK, LB, BLK, BLK), b_rows.reshape(NK * NK, LB), b_cols.reshape(NK * NK, LB), KP, CB)
    b_stored = b_stored.reshape(NK, NK, KP, CB, BLK, BLK)
    b_order = (panel_ids[:, None] - panel_ids[None, :]) % NK
    b_true = b_stored[b_order, panel_ids[None, :]]
    b_mat = b_true.transpose(0, 2, 4, 1, 3, 5).reshape(NK, KP * BLK, NB * BLK).astype(jnp.bfloat16)

    def one_band(inputs):
        a_band, keep_band = inputs

        def step(running, pieces):
            a_piece, b_piece, keep_piece = pieces
            product = jnp.dot(a_piece, b_piece, preferred_element_type=jnp.float32)
            product = product.reshape(RB, BLK, NB, BLK) * keep_piece.astype(jnp.float32)[:, None, :, None]
            return running + product.reshape(RB * BLK, NB * BLK), None

        start = jnp.zeros((RB * BLK, NB * BLK), jnp.float32)
        running, unused = lax.scan(step, start, (a_band, b_mat, keep_band.transpose(1, 0, 2)))
        return running

    c_sum = lax.map(one_band, (a_mat, prod_keep.reshape(BANDS, RB, NK, NB)))
    c_sum = c_sum.reshape(MB, BLK, NB, BLK) * res_keep.astype(jnp.float32)[:, None, :, None]
    return c_sum.reshape(MB * BLK, NB * BLK).astype(jnp.bfloat16)
```

```python
import jax
import jax.numpy as jnp
from jax import lax
from jax.experimental import pallas as pl
from jax.experimental.pallas import tpu as pltpu
from jax.sharding import PartitionSpec as P

BLK = 128
RB = 8
CB = 4
KP = 4
SIDE = 4
META = 16
HALF = 8
ROWS = HALF * BLK + META
BZERO = 16 * ROWS
STEPS = (1, -1, 2)


def with_meta(blocks, position):
    lanes = jnp.pad(position.astype(jnp.bfloat16), (0, BLK - position.shape[0]))
    meta = jnp.broadcast_to(lanes[None, :], (META, BLK))
    return jnp.concatenate([blocks.reshape(HALF * BLK, BLK), meta], axis=0)


def move_a(value, distance, phase):
    pairs = []
    for x in range(SIDE):
        for y in range(SIDE):
            for core in range(2):
                along_y = (core == 0) == (phase == 0)
                tx = x if along_y else (x + distance) % SIDE
                ty = (y + distance) % SIDE if along_y else y
                pairs.append(((x * SIDE + y) * 2 + core, (tx * SIDE + ty) * 2 + core))
    return lax.ppermute(value, ("row", "layer"), pairs)


def move_b(value, depth):
    pairs = []
    for z in range(depth):
        pairs.append((z * 2, ((z + 1) % depth) * 2))
        pairs.append((z * 2 + 1, ((z - 1) % depth) * 2 + 1))
    return lax.ppermute(value, ("col", "layer"), pairs)


def swap(value):
    return lax.ppermute(value, "layer", [(0, 1), (1, 0)])


def delta(index):
    return jnp.where(index == 0, 0, jnp.where(index == 1, SIDE - 1, index - 1))


def multiply(place, keep, *refs):
    a_refs, b_refs = refs[:4], refs[4:13]
    send, own, av, bv, acc, meta_v, meta_s, table, sem, meta_sem = refs[13:]
    x, y, z, core = place[0], place[1], place[2], place[3]
    copies = []
    for g in range(4):
        for m in range(4):
            p = 4 * g + m
            copies.append(
                pltpu.make_async_copy(a_refs[g].at[m], av.at[pl.ds(p * ROWS, ROWS)], sem.at[p])
            )
    copies.append(pltpu.make_async_copy(b_refs[0].at[0], bv.at[pl.ds(0, ROWS)], sem.at[16]))
    copies.append(pltpu.make_async_copy(b_refs[0].at[1], bv.at[pl.ds(ROWS, ROWS)], sem.at[17]))
    for t in range(1, 4):
        up = jnp.where(core == 0, 8 - t, t)
        down = jnp.where(core == 0, t, 8 - t)
        for i in range(2):
            copies.append(
                pltpu.make_async_copy(
                    b_refs[t].at[i],
                    bv.at[pl.ds(pl.multiple_of((up * 2 + i) * ROWS, META), ROWS)],
                    sem.at[16 + 4 * t - 2 + i],
                )
            )
            copies.append(
                pltpu.make_async_copy(
                    b_refs[3 + t].at[i],
                    bv.at[pl.ds(pl.multiple_of((down * 2 + i) * ROWS, META), ROWS)],
                    sem.at[16 + 4 * t + i],
                )
            )
    copies.append(
        pltpu.make_async_copy(
            b_refs[7].at[0], bv.at[pl.ds(pl.multiple_of((8 + core) * ROWS, META), ROWS)], sem.at[30]
        )
    )
    copies.append(
        pltpu.make_async_copy(
            b_refs[8].at[0], bv.at[pl.ds(pl.multiple_of((9 - core) * ROWS, META), ROWS)], sem.at[31]
        )
    )
    for copy in copies:
        copy.start()
    acc[...] = jnp.zeros_like(acc)
    bv[BZERO : BZERO + BLK, :] = jnp.zeros((BLK, BLK), jnp.bfloat16)
    for copy in copies:
        copy.wait()
    for p in range(16):
        for held, at in ((av, p), (bv, 16 + p)):
            tile = held[p * ROWS + HALF * BLK : (p + 1) * ROWS, :]
            meta_v[at : at + 1, :] = tile.astype(jnp.float32)[0:1, :].astype(jnp.int32)
    to_scalars = pltpu.make_async_copy(meta_v, meta_s, meta_sem)
    to_scalars.start()
    to_scalars.wait()

    def panel(p, carry):
        g, m = p // 4, p % 4
        first, second = delta(g), delta(m)
        px = (x + jnp.where(core == 0, first, second)) % SIDE
        py = (y + jnp.where(core == 0, second, first)) % SIDE
        k = (px * SIDE + py + 2 * z) % 16
        q = (k - (x * SIDE + y) + 16) % 16
        where_b = ((q // 2 - z + 8) % 8) * 2 + q % 2
        for i in range(KP * CB):
            table[i] = BZERO
        for t in range(HALF):
            table[meta_s[16 + where_b, t]] = where_b * ROWS + t * BLK
        for s in range(HALF):
            number = meta_s[p, s]
            live = number < RB * KP
            number = jnp.where(live, number, 0)
            r, c = number // KP, number % KP
            left = av[pl.ds(pl.multiple_of(p * ROWS + s * BLK, META), BLK), :]
            right = jnp.concatenate(
                [
                    bv[pl.ds(pl.multiple_of(table[c * CB + n], META), BLK), :]
                    for n in range(CB)
                ],
                axis=1,
            )
            product = jnp.dot(left, right, preferred_element_type=jnp.float32)
            for n in range(CB):
                kept = jnp.where(live, keep[r, k * CB + n], 0).astype(jnp.float32)
                cols = slice(n * BLK, (n + 1) * BLK)
                acc[r, :, cols] += product[:, cols] * kept
        return carry

    lax.fori_loop(0, 16, panel, 0)

    @pl.when(core == 0)
    def _():
        own[...] = acc[:, :, : 2 * BLK]
        send[...] = acc[:, :, 2 * BLK :]

    @pl.when(core != 0)
    def _():
        own[...] = acc[:, :, 2 * BLK :]
        send[...] = acc[:, :, : 2 * BLK]


def partial_sums(place, keep, a_parts, b_parts):
    vmem = pl.BlockSpec(memory_space=pltpu.VMEM)
    smem = pl.BlockSpec(memory_space=pltpu.SMEM)
    anywhere = pl.BlockSpec(memory_space=pl.ANY)
    half = jax.ShapeDtypeStruct((RB, BLK, 2 * BLK), jnp.float32)
    return pl.pallas_call(
        multiply,
        out_shape=(half, half),
        in_specs=[smem, smem] + [anywhere] * 13,
        out_specs=(vmem, vmem),
        scratch_shapes=[
            pltpu.VMEM((16 * ROWS, BLK), jnp.bfloat16),
            pltpu.VMEM((16 * ROWS + BLK, BLK), jnp.bfloat16),
            pltpu.VMEM((RB, BLK, CB * BLK), jnp.float32),
            pltpu.VMEM((32, BLK), jnp.int32),
            pltpu.SMEM((32, BLK), jnp.int32),
            pltpu.SMEM((32,), jnp.int32),
            pltpu.SemaphoreType.DMA((32,)),
            pltpu.SemaphoreType.DMA,
        ],
        compiler_params=pltpu.CompilerParams(vmem_limit_bytes=32 * 1024 * 1024),
    )(place, keep, *a_parts, *b_parts)


def body(a_blocks, a_rows, a_cols, b_blocks, b_rows, b_cols, prod_keep, res_keep):
    depth = lax.axis_size("col")
    row = lax.axis_index("row")
    z = lax.axis_index("col")
    core = lax.axis_index("layer")
    place = jnp.stack([row // SIDE, row % SIDE, z, core]).astype(jnp.int32)

    a_half = lax.dynamic_index_in_dim(
        a_blocks[0, 0].reshape(HALF, 2, BLK, BLK), core, 1, keepdims=False
    )
    a_number = (a_rows[0, 0] * KP + a_cols[0, 0]).reshape(HALF, 2)
    a_number = lax.dynamic_index_in_dim(a_number, core, 1, keepdims=False)
    a_mine = with_meta(a_half, a_number)
    b_number = b_rows[:, 0] * CB + b_cols[:, 0]
    b_mine = jnp.stack([with_meta(b_blocks[i, 0], b_number[i]) for i in range(2)])

    b_from = [b_mine]
    for _ in range(3):
        b_from.append(move_b(b_from[-1], depth))
    last = move_b(lax.dynamic_slice_in_dim(b_from[3], core, 1, 0), depth)
    b_theirs = [swap(part) for part in b_from[1:]]
    last_theirs = swap(last)

    a_own = jnp.stack([a_mine] + [move_a(a_mine, d, 0) for d in STEPS])
    a_parts = [a_own] + [move_a(a_own, d, 1) for d in STEPS]

    send, own = partial_sums(
        place,
        prod_keep.reshape(RB, 16 * CB),
        a_parts,
        b_from + b_theirs + [last, last_theirs],
    )
    total = own + swap(send)
    total = total.reshape(RB, BLK, 2, BLK) * res_keep.astype(jnp.float32)[:, None, :, None]
    return total.reshape(RB * BLK, 2 * BLK).astype(jnp.bfloat16)


def solution(mesh):
    return jax.shard_map(
        body,
        mesh=mesh,
        in_specs=(
            P("col", "row", None, None, None),
            P("col", "row", None),
            P("col", "row", None),
            P("col", "row", None, None, None),
            P("col", "row", None),
            P("col", "row", None),
            P("col", None, "row"),
            P("col", ("row", "layer")),
        ),
        out_specs=P("col", ("row", "layer")),
        check_vma=False,
    )
```

```python
import jax
import jax.numpy as jnp
from jax import lax
from jax.experimental import pallas as pl
from jax.experimental.pallas import tpu as pltpu
from jax.sharding import PartitionSpec as P

BLK = 128
RB = 8
CB = 4
KP = 4
SIDE = 4
META = 16
HALF = 8
DATA = HALF * BLK
ROWS = DATA + META
STEPS = (1, -1, 2)
ITEMS = 6
MOST = 64
LISTS = 8
NONE = 128 * 128


def with_meta(blocks, first, second):
    numbers = jnp.concatenate([first, second]).astype(jnp.bfloat16)
    meta = jnp.broadcast_to(numbers[:, None], (META, BLK))
    return jnp.concatenate([blocks.reshape(DATA, BLK), meta], axis=0)


def move_a(value, distance, phase):
    pairs = []
    for x in range(SIDE):
        for y in range(SIDE):
            for core in range(2):
                along_y = (core == 0) == (phase == 0)
                tx = x if along_y else (x + distance) % SIDE
                ty = (y + distance) % SIDE if along_y else y
                pairs.append(((x * SIDE + y) * 2 + core, (tx * SIDE + ty) * 2 + core))
    return lax.ppermute(value, ("row", "layer"), pairs)


def move_b(value, depth):
    pairs = []
    for z in range(depth):
        pairs.append((z * 2, ((z + 1) % depth) * 2))
        pairs.append((z * 2 + 1, ((z - 1) % depth) * 2 + 1))
    return lax.ppermute(value, ("col", "layer"), pairs)


def swap(value):
    return lax.ppermute(value, "layer", [(0, 1), (1, 0)])


def delta(index):
    return (0, SIDE - 1, 1, 2)[index]


def multiply(place, keep, *refs):
    a_refs, b_refs = refs[:4], refs[4:13]
    send, own, av, bv, am, bm, keys, list_v, lists, data_sem, meta_sem, list_sem = refs[13:]
    x, y, z, core = place[0], place[1], place[2], place[3]
    spots = [(b_refs[0], 0, 2)]
    for t in range(1, 4):
        spots.append((b_refs[t], 2 * jnp.where(core == 0, 8 - t, t), 2))
        spots.append((b_refs[3 + t], 2 * jnp.where(core == 0, t, 8 - t), 2))
    spots.append((b_refs[7], 8 + core, 1))
    spots.append((b_refs[8], 9 - core, 1))
    copies, metas = [], []
    for held, meta, group in (
        (av, am, [(a_refs[g], 4 * g, 4) for g in range(4)]),
        (bv, bm, spots),
    ):
        for ref, at, count in group:
            n = len(copies)
            copies.append(
                pltpu.make_async_copy(
                    ref.at[:, pl.ds(0, DATA), :], held.at[pl.ds(at, count)], data_sem.at[n]
                )
            )
            metas.append(
                pltpu.make_async_copy(
                    ref.at[:, pl.ds(DATA, META), :], meta.at[pl.ds(at, count)], meta_sem.at[n]
                )
            )
    for copy in metas:
        copy.start()
    for copy in copies:
        copy.start()
    av[16, 0:BLK, :] = jnp.zeros((BLK, BLK), jnp.bfloat16)
    lane = lax.broadcasted_iota(jnp.int32, (HALF, BLK), 1)
    slot = lax.broadcasted_iota(jnp.int32, (HALF, BLK), 0).astype(jnp.float32)
    bucket_row = (lane // CB).astype(jnp.float32)
    bucket_col = (lane % CB).astype(jnp.float32)
    for copy in metas:
        copy.wait()
    count = jnp.zeros((HALF, BLK), jnp.float32)
    for p in range(16):
        first, second = delta(p // 4), delta(p % 4)
        px = (x + jnp.where(core == 0, first, second)) % SIDE
        py = (y + jnp.where(core == 0, second, first)) % SIDE
        k = (px * SIDE + py + 2 * z) % 16
        q = (k - (x * SIDE + y) + 16) % 16
        spot = ((q // 2 - z + 8) % 8) * 2 + q % 2
        numbers = am[p].astype(jnp.float32)
        wanted = numbers[HALF:, :] + bucket_col
        b_numbers = bm[spot].astype(jnp.float32)
        found = jnp.zeros((HALF, BLK), jnp.float32)
        for t in range(HALF):
            found = jnp.where(b_numbers[t : t + 1, :] == wanted, t + 1.0, found)
        kept = keep[pl.ds(k, 1), :].astype(jnp.float32)
        valid = jnp.where(numbers[:HALF, :] == bucket_row, kept, 0.0)
        valid = (valid != 0.0) & (found != 0.0)
        base = (p * HALF * 128 - 1 + spot * HALF).astype(jnp.float32)
        keys[p] = jnp.where(valid, base + slot * 128.0 + found, float(NONE))
        count = count + jnp.where(valid, 1.0, 0.0)
    count = jnp.sum(count, axis=0, keepdims=True)
    list_v[0:1, :] = count.astype(jnp.int32)
    largest = jnp.max(count).astype(jnp.int32)

    def pick(j):
        least = keys[0]
        for p in range(1, 16):
            least = jnp.minimum(least, keys[p])
        least = jnp.min(least, axis=0, keepdims=True)
        list_v[pl.ds(1 + j, 1), :] = least.astype(jnp.int32)
        for p in range(16):
            keys[p] = jnp.where(keys[p] == least, float(NONE), keys[p])

    for j in range(ITEMS):
        pick(j)
    near = pltpu.make_async_copy(
        list_v.at[pl.ds(0, LISTS)], lists.at[pl.ds(0, LISTS)], list_sem.at[0]
    )
    near.start()
    near.wait()
    for copy in copies:
        copy.wait()

    def product(b, start, length):
        left, right = [], []
        for j in range(length):
            code = lists[1 + start + j, b]
            ia, ib = code // 128, code % 128
            left.append(av[ia // HALF, pl.ds(pl.multiple_of((ia % HALF) * BLK, BLK), BLK), :])
            right.append(bv[ib // HALF, pl.ds(pl.multiple_of((ib % HALF) * BLK, BLK), BLK), :])
        return jnp.dot(
            jnp.concatenate(left, axis=1),
            jnp.concatenate(right, axis=0),
            preferred_element_type=jnp.float32,
        )

    outs = ((send, 2 * (1 - core)), (own, 2 * core))

    def block_row(r, carry):
        for ref, base in outs:
            for n in range(2):
                ref[r, :, n * BLK : (n + 1) * BLK] = product(r * CB + base + n, 0, ITEMS)
        return carry

    lax.fori_loop(0, RB, block_row, 0)

    @pl.when(largest > ITEMS)
    def _():
        def more(j, carry):
            pick(j)
            return carry

        lax.fori_loop(ITEMS, largest, more, 0)
        far = pltpu.make_async_copy(list_v, lists, list_sem.at[1])
        far.start()
        far.wait()

        def rest_of_row(r, carry):
            for ref, base in outs:
                for n in range(2):
                    b = r * CB + base + n

                    def one(j, inner):
                        ref[r, :, n * BLK : (n + 1) * BLK] += product(b, j, 1)
                        return inner

                    lax.fori_loop(ITEMS, jnp.maximum(lists[0, b], ITEMS), one, 0)
            return carry

        lax.fori_loop(0, RB, rest_of_row, 0)


def partial_sums(place, keep, a_parts, b_parts):
    vmem = pl.BlockSpec(memory_space=pltpu.VMEM)
    smem = pl.BlockSpec(memory_space=pltpu.SMEM)
    anywhere = pl.BlockSpec(memory_space=pl.ANY)
    half = jax.ShapeDtypeStruct((RB, BLK, 2 * BLK), jnp.float32)
    return pl.pallas_call(
        multiply,
        out_shape=(half, half),
        in_specs=[smem, vmem] + [anywhere] * 13,
        out_specs=(vmem, vmem),
        scratch_shapes=[
            pltpu.VMEM((17, DATA, BLK), jnp.bfloat16),
            pltpu.VMEM((16, DATA, BLK), jnp.bfloat16),
            pltpu.VMEM((16, META, BLK), jnp.bfloat16),
            pltpu.VMEM((16, META, BLK), jnp.bfloat16),
            pltpu.VMEM((16, HALF, BLK), jnp.float32),
            pltpu.VMEM((LISTS + MOST, BLK), jnp.int32),
            pltpu.SMEM((LISTS + MOST, BLK), jnp.int32),
            pltpu.SemaphoreType.DMA((13,)),
            pltpu.SemaphoreType.DMA((13,)),
            pltpu.SemaphoreType.DMA((2,)),
        ],
        compiler_params=pltpu.CompilerParams(vmem_limit_bytes=32 * 1024 * 1024),
    )(place, keep, *a_parts, *b_parts)


def finish(keep, own, other, out):
    for r in range(RB):
        for n in range(2):
            cols = slice(n * BLK, (n + 1) * BLK)
            total = own[r, :, cols] + other[r, :, cols]
            total = total * keep[r, n].astype(jnp.float32)
            out[r * BLK : (r + 1) * BLK, cols] = total.astype(jnp.bfloat16)


def filtered(keep, own, other):
    vmem = pl.BlockSpec(memory_space=pltpu.VMEM)
    return pl.pallas_call(
        finish,
        out_shape=jax.ShapeDtypeStruct((RB * BLK, 2 * BLK), jnp.bfloat16),
        in_specs=[pl.BlockSpec(memory_space=pltpu.SMEM), vmem, vmem],
        out_specs=vmem,
    )(keep, own, other)


def body(a_blocks, a_rows, a_cols, b_blocks, b_rows, b_cols, prod_keep, res_keep):
    depth = lax.axis_size("col")
    row = lax.axis_index("row")
    z = lax.axis_index("col")
    core = lax.axis_index("layer")
    place = jnp.stack([row // SIDE, row % SIDE, z, core]).astype(jnp.int32)

    def my_half(array):
        halves = array.reshape((HALF, 2) + array.shape[1:])
        return lax.dynamic_index_in_dim(halves, core, 1, keepdims=False)

    a_mine = with_meta(my_half(a_blocks[0, 0]), my_half(a_rows[0, 0]), my_half(a_cols[0, 0]) * CB)
    b_number = b_rows[:, 0] * CB + b_cols[:, 0]
    b_mine = jnp.stack([with_meta(b_blocks[i, 0], b_number[i], b_number[i]) for i in range(2)])

    b_from = [b_mine]
    for _ in range(3):
        b_from.append(move_b(b_from[-1], depth))
    last = move_b(lax.dynamic_slice_in_dim(b_from[3], core, 1, 0), depth)
    b_theirs = [swap(part) for part in b_from[1:]]
    last_theirs = swap(last)

    a_own = jnp.stack([a_mine] + [move_a(a_mine, d, 0) for d in STEPS])
    a_parts = [a_own] + [move_a(a_own, d, 1) for d in STEPS]

    keep = prod_keep.transpose(1, 0, 2).reshape(16, RB * CB)
    keep = jnp.pad(keep, ((0, 0), (0, BLK - RB * CB)))
    send, own = partial_sums(place, keep, a_parts, b_from + b_theirs + [last, last_theirs])
    return filtered(res_keep, own, swap(send))


def solution(mesh):
    return jax.shard_map(
        body,
        mesh=mesh,
        in_specs=(
            P("col", "row", None, None, None),
            P("col", "row", None),
            P("col", "row", None),
            P("col", "row", None, None, None),
            P("col", "row", None),
            P("col", "row", None),
            P("col", None, "row"),
            P("col", ("row", "layer")),
        ),
        out_specs=P("col", ("row", "layer")),
        check_vma=False,
    )
```

```python
import functools

import jax
import jax.numpy as jnp
from jax import lax
from jax.experimental import pallas as pl
from jax.experimental.pallas import tpu as pltpu
from jax.sharding import PartitionSpec as P

BLK = 128
RB = 8
CB = 4
KP = 4
SIDE = 4
META = 16
HALF = 8
DATA = HALF * BLK
ROWS = DATA + META
MOST = 64
LISTS = 8
NONE = 128 * 128
DELTA = (0, SIDE - 1, 1, 2)
LIMIT = 60 * 1024 * 1024


def move_a(value, distance, phase):
    pairs = []
    for x in range(SIDE):
        for y in range(SIDE):
            for core in range(2):
                along_y = (core == 0) == (phase == 0)
                tx = x if along_y else (x + distance) % SIDE
                ty = (y + distance) % SIDE if along_y else y
                pairs.append(((x * SIDE + y) * 2 + core, (tx * SIDE + ty) * 2 + core))
    return lax.ppermute(value, ("row", "layer"), pairs)


def move_b(value, depth):
    pairs = []
    for z in range(depth):
        pairs.append((z * 2, ((z + 1) % depth) * 2))
        pairs.append((z * 2 + 1, ((z - 1) % depth) * 2 + 1))
    return lax.ppermute(value, ("col", "layer"), pairs)


def swap(value):
    return lax.ppermute(value, "layer", [(0, 1), (1, 0)])


def pack(a_rows, a_cols, b_rows, b_cols, a_blocks, b_blocks, a_out, b_first, b_second, sem):
    core = lax.axis_index("layer")
    copies = []
    for s in range(HALF):
        copies.append(
            pltpu.make_async_copy(
                a_blocks.at[0, 0, 2 * s + core], a_out.at[pl.ds(s * BLK, BLK)], sem.at[s]
            )
        )
    for i, out in enumerate((b_first, b_second)):
        for t in range(HALF):
            copies.append(
                pltpu.make_async_copy(
                    b_blocks.at[i, 0, t], out.at[pl.ds(t * BLK, BLK)], sem.at[8 + 8 * i + t]
                )
            )
    for copy in copies:
        copy.start()
    line = lax.broadcasted_iota(jnp.int32, (META, BLK), 0)
    numbers = jnp.zeros((META, BLK), jnp.int32)
    for s in range(HALF):
        numbers = jnp.where(line == s, a_rows[0, 0, 2 * s + core], numbers)
        numbers = jnp.where(line == HALF + s, a_cols[0, 0, 2 * s + core] * CB, numbers)
    a_out[DATA:ROWS, :] = numbers.astype(jnp.float32).astype(jnp.bfloat16)
    for i, out in enumerate((b_first, b_second)):
        numbers = jnp.zeros((META, BLK), jnp.int32)
        for t in range(HALF):
            numbers = jnp.where(line == t, b_rows[i, 0, t] * CB + b_cols[i, 0, t], numbers)
        out[DATA:ROWS, :] = numbers.astype(jnp.float32).astype(jnp.bfloat16)
    for copy in copies:
        copy.wait()


def packed(a_blocks, a_rows, a_cols, b_blocks, b_rows, b_cols):
    vmem = pl.BlockSpec(memory_space=pltpu.VMEM)
    smem = pl.BlockSpec(memory_space=pltpu.SMEM)
    anywhere = pl.BlockSpec(memory_space=pl.ANY)
    tile = jax.ShapeDtypeStruct((ROWS, BLK), jnp.bfloat16)
    return pl.pallas_call(
        pack,
        out_shape=(tile, tile, tile),
        in_specs=[smem] * 4 + [anywhere] * 2,
        out_specs=(vmem,) * 3,
        scratch_shapes=[pltpu.SemaphoreType.DMA((24,))],
        name="pack",
    )(a_rows, a_cols, b_rows, b_cols, a_blocks, b_blocks)


def multiply(groups, items, from_tiles, added, place, keep, *refs):
    x, y, z, core = place[0], place[1], place[2], place[3]
    panels = [(g, m) for g, ms in groups for m in ms]
    n_a = len(groups)
    a_refs, refs = refs[:n_a], refs[n_a:]
    n_b = 1 if from_tiles else 16
    b_refs, refs = refs[:n_b], refs[n_b:]
    if added:
        (send_in, own_in), refs = refs[:2], refs[2:]
    send, own = refs[:2]
    refs = refs[2:]
    if not from_tiles:
        tiles, refs = refs[0], refs[1:]
    av, bv, am, bm, keys, list_v, lists, data_sem, meta_sem, list_sem, add_sem = refs
    spots = []
    for p, (g, m) in enumerate(panels):
        px = (x + jnp.where(core == 0, DELTA[g], DELTA[m])) % SIDE
        py = (y + jnp.where(core == 0, DELTA[m], DELTA[g])) % SIDE
        k = (px * SIDE + py + 2 * z) % 16
        q = (k - (x * SIDE + y) + 16) % 16
        spots.append((k, ((q // 2 - z + 8) % 8) * 2 + q % 2))
    sources = []
    at = 0
    for (g, ms), ref in zip(groups, a_refs):
        sources.append((ref, av, am, at, len(ms)))
        at += len(ms)
    if from_tiles:
        for p, (k, spot) in enumerate(spots):
            sources.append((b_refs[0].at[pl.ds(spot, 1)], bv, bm, p, 1))
    else:
        sources.append((b_refs[0], bv, bm, 0, 1))
        sources.append((b_refs[1], bv, bm, 1, 1))
        for t in range(1, 4):
            for i in range(2):
                up = 2 * jnp.where(core == 0, 8 - t, t) + i
                down = 2 * jnp.where(core == 0, t, 8 - t) + i
                sources.append((b_refs[2 * t + i], bv, bm, up, 1))
                sources.append((b_refs[6 + 2 * t + i], bv, bm, down, 1))
        sources.append((b_refs[14], bv, bm, 8 + core, 1))
        sources.append((b_refs[15], bv, bm, 9 - core, 1))
    copies, metas = [], []
    for n, (ref, held, meta, at, count) in enumerate(sources):
        copies.append(
            pltpu.make_async_copy(
                ref.at[:, pl.ds(0, DATA), :], held.at[pl.ds(at, count)], data_sem.at[n]
            )
        )
        metas.append(
            pltpu.make_async_copy(
                ref.at[:, pl.ds(DATA, META), :], meta.at[pl.ds(at, count)], meta_sem.at[n]
            )
        )
    for copy in metas:
        copy.start()
    for copy in copies:
        copy.start()
    if added:
        adds = [
            pltpu.make_async_copy(send_in, send, add_sem.at[0]),
            pltpu.make_async_copy(own_in, own, add_sem.at[1]),
        ]
        for copy in adds:
            copy.start()
    none_a = len(panels)
    av[none_a, 0:BLK, :] = jnp.zeros((BLK, BLK), jnp.bfloat16)
    none = float(none_a * HALF * 128)
    lane = lax.broadcasted_iota(jnp.int32, (HALF, BLK), 1)
    slot = lax.broadcasted_iota(jnp.int32, (HALF, BLK), 0).astype(jnp.float32)
    bucket_row = (lane // CB).astype(jnp.float32)
    bucket_col = (lane % CB).astype(jnp.float32)
    for copy in metas:
        copy.wait()
    count = jnp.zeros((HALF, BLK), jnp.float32)
    for p, (k, spot) in enumerate(spots):
        if from_tiles:
            spot = jnp.int32(p)
        numbers = am[p].astype(jnp.float32)
        wanted = numbers[HALF:, :] + bucket_col
        b_numbers = bm[spot].astype(jnp.float32)
        found = jnp.zeros((HALF, BLK), jnp.float32)
        for t in range(HALF):
            found = jnp.where(b_numbers[t : t + 1, :] == wanted, t + 1.0, found)
        kept = keep[pl.ds(k, 1), :].astype(jnp.float32)
        valid = jnp.where(numbers[:HALF, :] == bucket_row, kept, 0.0)
        valid = (valid != 0.0) & (found != 0.0)
        base = (p * HALF * 128 - 1 + spot * HALF).astype(jnp.float32)
        keys[p] = jnp.where(valid, base + slot * 128.0 + found, none)
        count = count + jnp.where(valid, 1.0, 0.0)
    count = jnp.sum(count, axis=0, keepdims=True)
    list_v[0:1, :] = count.astype(jnp.int32)
    largest = jnp.max(count).astype(jnp.int32)

    def pick(j):
        least = keys[0]
        for p in range(1, len(panels)):
            least = jnp.minimum(least, keys[p])
        least = jnp.min(least, axis=0, keepdims=True)
        list_v[pl.ds(1 + j, 1), :] = least.astype(jnp.int32)
        for p in range(len(panels)):
            keys[p] = jnp.where(keys[p] == least, none, keys[p])

    for j in range(items):
        pick(j)
    near = pltpu.make_async_copy(
        list_v.at[pl.ds(0, LISTS)], lists.at[pl.ds(0, LISTS)], list_sem.at[0]
    )
    near.start()
    near.wait()
    for copy in copies:
        copy.wait()
    if added:
        for copy in adds:
            copy.wait()
    else:
        keeping = pltpu.make_async_copy(bv, tiles.at[:, pl.ds(0, DATA), :], add_sem.at[0])
        keeping.start()
        keeping_meta = pltpu.make_async_copy(bm, tiles.at[:, pl.ds(DATA, META), :], add_sem.at[1])
        keeping_meta.start()

    def product(b, start, length):
        left, right = [], []
        for j in range(length):
            code = lists[1 + start + j, b]
            ia, ib = code // 128, code % 128
            left.append(av[ia // HALF, pl.ds(pl.multiple_of((ia % HALF) * BLK, BLK), BLK), :])
            right.append(bv[ib // HALF, pl.ds(pl.multiple_of((ib % HALF) * BLK, BLK), BLK), :])
        return jnp.dot(
            jnp.concatenate(left, axis=1),
            jnp.concatenate(right, axis=0),
            preferred_element_type=jnp.float32,
        )

    outs = ((send, 2 * (1 - core)), (own, 2 * core))
    for r in range(RB):
        for ref, base in outs:
            for n in range(2):
                cols = slice(n * BLK, (n + 1) * BLK)
                result = product(r * CB + base + n, 0, items)
                ref[r, :, cols] = ref[r, :, cols] + result if added else result

    @pl.when(largest > items)
    def _():
        def more(j, carry):
            pick(j)
            return carry

        lax.fori_loop(items, largest, more, 0)
        far = pltpu.make_async_copy(list_v, lists, list_sem.at[1])
        far.start()
        far.wait()

        def rest_of_row(r, carry):
            for ref, base in outs:
                for n in range(2):
                    b = r * CB + base + n

                    def one(j, inner):
                        ref[r, :, n * BLK : (n + 1) * BLK] += product(b, j, 1)
                        return inner

                    lax.fori_loop(items, jnp.maximum(lists[0, b], items), one, 0)
            return carry

        lax.fori_loop(0, RB, rest_of_row, 0)

    if not added:
        keeping.wait()
        keeping_meta.wait()


def partial_sums(place, keep, groups, items, a_parts, b_parts, before=None):
    vmem = pl.BlockSpec(memory_space=pltpu.VMEM)
    smem = pl.BlockSpec(memory_space=pltpu.SMEM)
    anywhere = pl.BlockSpec(memory_space=pl.ANY)
    n_panels = sum(len(ms) for _, ms in groups)
    added = before is not None
    n_b = n_panels if added else 16
    half = jax.ShapeDtypeStruct((RB, BLK, 2 * BLK), jnp.float32)
    out_shape, out_specs = [half, half], [vmem, vmem]
    if not added:
        out_shape.append(jax.ShapeDtypeStruct((16, ROWS, BLK), jnp.bfloat16))
        out_specs.append(anywhere)
    extra = list(before) if added else []
    n_sources = len(a_parts) + (n_panels if added else 16)
    return pl.pallas_call(
        functools.partial(multiply, groups, items, added, added),
        out_shape=out_shape,
        in_specs=[smem, vmem] + [anywhere] * (len(a_parts) + len(b_parts) + len(extra)),
        out_specs=out_specs,
        scratch_shapes=[
            pltpu.VMEM((n_panels + 1, DATA, BLK), jnp.bfloat16),
            pltpu.VMEM((n_b, DATA, BLK), jnp.bfloat16),
            pltpu.VMEM((n_panels, META, BLK), jnp.bfloat16),
            pltpu.VMEM((n_b, META, BLK), jnp.bfloat16),
            pltpu.VMEM((n_panels, HALF, BLK), jnp.float32),
            pltpu.VMEM((LISTS + MOST, BLK), jnp.int32),
            pltpu.SMEM((LISTS + MOST, BLK), jnp.int32),
            pltpu.SemaphoreType.DMA((n_sources,)),
            pltpu.SemaphoreType.DMA((n_sources,)),
            pltpu.SemaphoreType.DMA((2,)),
            pltpu.SemaphoreType.DMA((2,)),
        ],
        compiler_params=pltpu.CompilerParams(vmem_limit_bytes=LIMIT),
        name="late" if added else "early",
    )(place, keep, *a_parts, *b_parts, *extra)


def finish(keep, own, other, out):
    for r in range(RB):
        for n in range(2):
            cols = slice(n * BLK, (n + 1) * BLK)
            total = own[r, :, cols] + other[r, :, cols]
            total = total * keep[r, n].astype(jnp.float32)
            out[r * BLK : (r + 1) * BLK, cols] = total.astype(jnp.bfloat16)


def filtered(keep, own, other):
    vmem = pl.BlockSpec(memory_space=pltpu.VMEM)
    return pl.pallas_call(
        finish,
        out_shape=jax.ShapeDtypeStruct((RB * BLK, 2 * BLK), jnp.bfloat16),
        in_specs=[pl.BlockSpec(memory_space=pltpu.SMEM), vmem, vmem],
        out_specs=vmem,
        compiler_params=pltpu.CompilerParams(vmem_limit_bytes=LIMIT),
        name="finish",
    )(keep, own, other)


def body(a_blocks, a_rows, a_cols, b_blocks, b_rows, b_cols, prod_keep, res_keep):
    depth = lax.axis_size("col")
    row = lax.axis_index("row")
    z = lax.axis_index("col")
    core = lax.axis_index("layer")
    place = jnp.stack([row // SIDE, row % SIDE, z, core]).astype(jnp.int32)
    keep = prod_keep.transpose(1, 0, 2).reshape(16, RB * CB)
    keep = jnp.pad(keep, ((0, 0), (0, BLK - RB * CB)))

    a_mine, b_first, b_second = packed(a_blocks, a_rows, a_cols, b_blocks, b_rows, b_cols)

    mine = [[b_first[None], b_second[None]]]
    for _ in range(3):
        mine.append([move_b(part, depth) for part in mine[-1]])
    last = move_b(jnp.where(core == 0, mine[3][0], mine[3][1]), depth)
    theirs = [[swap(part) for part in pair] for pair in mine[1:]]
    b_parts = [part for pair in mine + theirs for part in pair] + [last, swap(last)]

    a_own = jnp.stack([a_mine] + [move_a(a_mine, d, 0) for d in (1, -1, 2)])
    a_up, a_down = move_a(a_own, 1, 1), move_a(a_own, -1, 1)
    a_far = [move_a(a_up[:2], 1, 1), move_a(a_down[2:], -1, 1)]

    whole = (0, 1, 2, 3)
    send, own, tiles = partial_sums(
        place, keep, ((0, whole), (1, whole), (2, whole)), 4, [a_own, a_up, a_down], b_parts
    )
    send, own = partial_sums(
        place, keep, ((3, (0, 1)), (3, (2, 3))), 2, a_far, [tiles], (send, own)
    )
    return filtered(res_keep, own, swap(send))


def solution(mesh):
    return jax.shard_map(
        body,
        mesh=mesh,
        in_specs=(
            P("col", "row", None, None, None),
            P("col", "row", None),
            P("col", "row", None),
            P("col", "row", None, None, None),
            P("col", "row", None),
            P("col", "row", None),
            P("col", None, "row"),
            P("col", ("row", "layer")),
        ),
        out_specs=P("col", ("row", "layer")),
        check_vma=False,
    )
```

```python
import jax
import jax.numpy as jnp
from jax import lax
from jax.experimental import pallas as pl
from jax.experimental.pallas import tpu as pltpu
from jax.sharding import PartitionSpec as P

BLK = 128
RB = 8
CB = 4
KP = 4
SIDE = 4
META = 16
HALF = 8
DATA = HALF * BLK
ROWS = DATA + META
MOST = 64
PICKS = 8
NEAR = 16
LISTS = 80
STEP = 8
BUCKETS = 32
NONE = 128
DELTA = (0, SIDE - 1, 1, 2)
STEPS = (1, -1, 2)


def move_a(value, distance, phase):
    pairs = []
    for x in range(SIDE):
        for y in range(SIDE):
            for core in range(2):
                along_y = (core == 0) == (phase == 0)
                tx = x if along_y else (x + distance) % SIDE
                ty = (y + distance) % SIDE if along_y else y
                pairs.append(((x * SIDE + y) * 2 + core, (tx * SIDE + ty) * 2 + core))
    return lax.ppermute(value, ("row", "layer"), pairs)


def move_b(value, distance, depth):
    pairs = []
    for z in range(depth):
        pairs.append((z * 2, ((z + distance) % depth) * 2))
        pairs.append((z * 2 + 1, ((z - distance) % depth) * 2 + 1))
    return lax.ppermute(value, ("col", "layer"), pairs)


def swap(value):
    return lax.ppermute(value, "layer", [(0, 1), (1, 0)])


def pack(
    a_rows, a_cols, b_rows, b_cols, a_blocks, b_blocks, a_out, b_out, ar, ac, br, bc, sem, num_sem
):
    core = lax.axis_index("layer")
    numbers = [
        pltpu.make_async_copy(source, held, num_sem.at[n])
        for n, (source, held) in enumerate(
            ((a_rows, ar), (a_cols, ac), (b_rows, br), (b_cols, bc))
        )
    ]
    for copy in numbers:
        copy.start()
    copies = []
    for i in range(2):
        for t in range(HALF):
            copies.append(
                pltpu.make_async_copy(
                    b_blocks.at[i, 0, t], b_out.at[i, pl.ds(t * BLK, BLK)], sem.at[8 * i + t]
                )
            )
    for s in range(HALF):
        copies.append(
            pltpu.make_async_copy(
                a_blocks.at[0, 0, 2 * s + core], a_out.at[pl.ds(s * BLK, BLK)], sem.at[16 + s]
            )
        )
    for copy in copies:
        copy.start()
    for copy in numbers:
        copy.wait()
    line = lax.broadcasted_iota(jnp.int32, (META, BLK), 0)
    tile = jnp.zeros((META, BLK), jnp.int32)
    for s in range(HALF):
        tile = jnp.where(line == s, ar[0, 0, 2 * s + core], tile)
        tile = jnp.where(line == HALF + s, ac[0, 0, 2 * s + core] * CB, tile)
    a_out[DATA:ROWS, :] = tile.astype(jnp.float32).astype(jnp.bfloat16)
    for i in range(2):
        tile = jnp.zeros((META, BLK), jnp.int32)
        for t in range(HALF):
            tile = jnp.where(line == t, br[i, 0, t] * CB + bc[i, 0, t], tile)
        b_out[i, DATA:ROWS, :] = tile.astype(jnp.float32).astype(jnp.bfloat16)
    for copy in copies:
        copy.wait()


def packed(a_blocks, a_rows, a_cols, b_blocks, b_rows, b_cols):
    vmem = pl.BlockSpec(memory_space=pltpu.VMEM)
    anywhere = pl.BlockSpec(memory_space=pl.ANY)
    return pl.pallas_call(
        pack,
        out_shape=(
            jax.ShapeDtypeStruct((ROWS, BLK), jnp.bfloat16),
            jax.ShapeDtypeStruct((2, ROWS, BLK), jnp.bfloat16),
        ),
        in_specs=[anywhere] * 6,
        out_specs=(vmem,) * 2,
        scratch_shapes=[
            pltpu.SMEM((1, 1, 16), jnp.int32),
            pltpu.SMEM((1, 1, 16), jnp.int32),
            pltpu.SMEM((2, 1, HALF), jnp.int32),
            pltpu.SMEM((2, 1, HALF), jnp.int32),
            pltpu.SemaphoreType.DMA((24,)),
            pltpu.SemaphoreType.DMA((4,)),
        ],
        compiler_params=pltpu.CompilerParams(vmem_limit_bytes=4 * 1024 * 1024),
        name="pack",
    )(
        *[
            pltpu.with_memory_space_constraint(part, pltpu.HBM)
            for part in (a_rows, a_cols, b_rows, b_cols, a_blocks, b_blocks)
        ]
    )


def read_numbers(*refs):
    out, sem = refs[3:]
    copies = [
        pltpu.make_async_copy(ref.at[:, pl.ds(DATA, META), :], out.at[pl.ds(4 * g, 4)], sem.at[g])
        for g, ref in enumerate(refs[:3])
    ]
    for copy in copies:
        copy.start()
    for copy in copies:
        copy.wait()


def numbers_of(parts):
    return pl.pallas_call(
        read_numbers,
        out_shape=jax.ShapeDtypeStruct((12, META, BLK), jnp.bfloat16),
        in_specs=[pl.BlockSpec(memory_space=pl.ANY)] * 3,
        out_specs=pl.BlockSpec(memory_space=pltpu.VMEM),
        scratch_shapes=[pltpu.SemaphoreType.DMA((3,))],
        cost_estimate=pl.CostEstimate(flops=10000000000, bytes_accessed=0, transcendentals=0),
        compiler_params=pltpu.CompilerParams(vmem_limit_bytes=4 * 1024 * 1024),
        name="numbers",
    )(*parts)


def multiply(keep, far_numbers, *refs):
    a_refs, b_refs = refs[:4], refs[4:13]
    send, own, av, bv, am, bm, acc, keys, list_v, lists, flat = refs[13:24]
    data_sem, meta_sem, list_sem = refs[24:]
    row, z, core = lax.axis_index("row"), lax.axis_index("col"), lax.axis_index("layer")
    x, y = row // SIDE, row % SIDE
    spots = [(b_refs[0], 0, 2)]
    for t in range(1, 4):
        spots.append((b_refs[t], 2 * jnp.where(core == 0, 8 - t, t), 2))
        spots.append((b_refs[3 + t], 2 * jnp.where(core == 0, t, 8 - t), 2))
    spots.append((b_refs[7], 8 + core, 1))
    spots.append((b_refs[8], 9 - core, 1))
    copies, metas = [], []
    for held, meta, group in (
        (av, am, [(a_refs[g], 4 * g, 4) for g in range(4)]),
        (bv, bm, spots),
    ):
        for ref, at, count in group:
            n = len(copies)
            whole = 1 <= n <= 3
            copies.append(
                pltpu.make_async_copy(
                    ref.at[:, pl.ds(0, DATA), :], held.at[pl.ds(at, count)], data_sem.at[n]
                )
            )
            if whole:
                continue
            metas.append(
                pltpu.make_async_copy(
                    ref.at[:, pl.ds(DATA, META), :], meta.at[pl.ds(at, count)], meta_sem.at[n]
                )
            )
    for copy in metas:
        copy.start()
    for copy in copies:
        copy.start()
    av[16, 0:BLK, :] = jnp.zeros((BLK, BLK), jnp.bfloat16)
    acc[...] = jnp.zeros_like(acc)
    none = float(NONE * 128)
    lane = lax.broadcasted_iota(jnp.int32, (HALF, BLK), 1)
    slot = lax.broadcasted_iota(jnp.int32, (HALF, BLK), 0).astype(jnp.float32)
    bucket_row = (lane // CB).astype(jnp.float32)
    bucket_col = (lane % CB).astype(jnp.float32)
    for copy in metas:
        copy.wait()
    count = jnp.zeros((HALF, BLK), jnp.float32)
    for p in range(16):
        first, second = DELTA[p // 4], DELTA[p % 4]
        px = (x + jnp.where(core == 0, first, second)) % SIDE
        py = (y + jnp.where(core == 0, second, first)) % SIDE
        k = (px * SIDE + py + 2 * z) % 16
        q = (k - row + 16) % 16
        spot = ((q // 2 - z + 8) % 8) * 2 + q % 2
        numbers = (am[p] if p < 4 else far_numbers[p - 4]).astype(jnp.float32)
        wanted = numbers[HALF:, :] + bucket_col
        b_numbers = bm[spot].astype(jnp.float32)
        found = jnp.zeros((HALF, BLK), jnp.float32)
        for t in range(HALF):
            found = jnp.where(b_numbers[t : t + 1, :] == wanted, t + 1.0, found)
        kept = keep[pl.ds(k, 1), :].astype(jnp.float32)
        valid = jnp.where(numbers[:HALF, :] == bucket_row, kept, 0.0)
        valid = (valid != 0.0) & (found != 0.0)
        base = (p * HALF * 128 - 1 + spot * HALF).astype(jnp.float32)
        keys[p] = jnp.where(valid, base + slot * 128.0 + found, none)
        count = count + jnp.where(valid, 1.0, 0.0)
    count = jnp.sum(count, axis=0, keepdims=True)
    list_v[0:1, :] = count.astype(jnp.int32)
    largest = jnp.max(count).astype(jnp.int32)

    def pick(j):
        least = keys[0]
        for p in range(1, 16):
            least = jnp.minimum(least, keys[p])
        least = jnp.min(least, axis=0, keepdims=True)
        list_v[pl.ds(1 + j, 1), :] = least.astype(jnp.int32)
        for p in range(16):
            keys[p] = jnp.where(keys[p] == least, none, keys[p])

    for j in range(PICKS):
        pick(j)
    first_part = pltpu.make_async_copy(
        list_v.at[pl.ds(0, NEAR)], lists.at[pl.ds(0, NEAR)], list_sem.at[0]
    )
    first_part.start()
    first_part.wait()

    @pl.when(largest > PICKS)
    def _():
        def more(j, carry):
            pick(j)
            return carry

        lax.fori_loop(PICKS, largest, more, 0)
        whole = pltpu.make_async_copy(list_v, lists, list_sem.at[1])
        whole.start()
        whole.wait()

    def bucket(b, n):
        length = lists[0, b]
        for j in range(4):
            flat[n + j] = lists[1 + j, b] * BUCKETS + b

        def item(j, carry):
            flat[n + j] = lists[1 + j, b] * BUCKETS + b
            return carry

        lax.fori_loop(4, jnp.maximum(length, 4), item, 0)
        return n + length

    total = lax.fori_loop(0, BUCKETS, bucket, 0, unroll=4)
    for j in range(STEP):
        flat[total + j] = NONE * 128 * BUCKETS
    for copy in copies:
        copy.wait()

    def step(i, carry):
        for j in range(STEP):
            code = flat[i * STEP + j]
            b, code = code % BUCKETS, code // BUCKETS
            ia, ib = code // 128, code % 128
            left = av[ia // HALF, pl.ds(pl.multiple_of((ia % HALF) * BLK, BLK), BLK), :]
            right = bv[ib // HALF, pl.ds(pl.multiple_of((ib % HALF) * BLK, BLK), BLK), :]
            acc[b] += jnp.dot(left, right, preferred_element_type=jnp.float32)
        return carry

    lax.fori_loop(0, (total + STEP - 1) // STEP, step, 0)
    for r in range(RB):
        for n in range(2):
            send[2 * r + n] = acc[r * CB + 2 * (1 - core) + n]
            own[2 * r + n] = acc[r * CB + 2 * core + n]


def partial_sums(keep, a_parts, b_parts):
    vmem = pl.BlockSpec(memory_space=pltpu.VMEM)
    anywhere = pl.BlockSpec(memory_space=pl.ANY)
    half = jax.ShapeDtypeStruct((2 * RB, BLK, BLK), jnp.float32)
    return pl.pallas_call(
        multiply,
        out_shape=(half, half),
        in_specs=[vmem, vmem] + [anywhere] * 13,
        out_specs=(vmem, vmem),
        scratch_shapes=[
            pltpu.VMEM((17, DATA, BLK), jnp.bfloat16),
            pltpu.VMEM((16, DATA, BLK), jnp.bfloat16),
            pltpu.VMEM((4, META, BLK), jnp.bfloat16),
            pltpu.VMEM((16, META, BLK), jnp.bfloat16),
            pltpu.VMEM((BUCKETS, BLK, BLK), jnp.float32),
            pltpu.VMEM((16, HALF, BLK), jnp.float32),
            pltpu.VMEM((LISTS, BLK), jnp.int32),
            pltpu.SMEM((LISTS, BLK), jnp.int32),
            pltpu.SMEM((BUCKETS * MOST + 2 * STEP,), jnp.int32),
            pltpu.SemaphoreType.DMA((13,)),
            pltpu.SemaphoreType.DMA((13,)),
            pltpu.SemaphoreType.DMA((2,)),
        ],
        compiler_params=pltpu.CompilerParams(vmem_limit_bytes=28 * 1024 * 1024),
        name="multiply",
    )(keep, numbers_of(a_parts[1:]), *a_parts, *b_parts)


def finish(keep, own, other, out):
    for r in range(RB):
        for n in range(2):
            total = (own[2 * r + n] + other[2 * r + n]) * keep[r, n].astype(jnp.float32)
            out[r * BLK : (r + 1) * BLK, n * BLK : (n + 1) * BLK] = total.astype(jnp.bfloat16)


def filtered(keep, own, other):
    vmem = pl.BlockSpec(memory_space=pltpu.VMEM)
    return pl.pallas_call(
        finish,
        out_shape=jax.ShapeDtypeStruct((RB * BLK, 2 * BLK), jnp.bfloat16),
        in_specs=[pl.BlockSpec(memory_space=pltpu.SMEM), vmem, vmem],
        out_specs=vmem,
        name="finish",
    )(keep, own, other)


def body(a_blocks, a_rows, a_cols, b_blocks, b_rows, b_cols, prod_keep, res_keep):
    depth = lax.axis_size("col")
    core = lax.axis_index("layer")
    keep = prod_keep.transpose(1, 0, 2).reshape(16, RB * CB)
    keep = jnp.pad(keep, ((0, 0), (0, BLK - RB * CB)))

    a_mine, b_mine = packed(a_blocks, a_rows, a_cols, b_blocks, b_rows, b_cols)

    b_from = [b_mine, move_b(b_mine, 1, depth), move_b(b_mine, 2, depth)]
    b_from.append(move_b(b_from[2], 1, depth))
    last = move_b(jnp.where(core == 0, b_from[2][:1], b_from[2][1:]), 2, depth)
    b_theirs = [swap(part) for part in b_from[1:]]

    a_own = jnp.stack([a_mine] + [move_a(a_mine, d, 0) for d in STEPS])
    a_parts = [a_own] + [move_a(a_own, d, 1) for d in STEPS]

    send, own = partial_sums(keep, a_parts, b_from + b_theirs + [last, swap(last)])
    return filtered(res_keep, own, swap(send))


def solution(mesh):
    return jax.shard_map(
        body,
        mesh=mesh,
        in_specs=(
            P("col", "row", None, None, None),
            P("col", "row", None),
            P("col", "row", None),
            P("col", "row", None, None, None),
            P("col", "row", None),
            P("col", "row", None),
            P("col", None, "row"),
            P("col", ("row", "layer")),
        ),
        out_specs=P("col", ("row", "layer")),
        check_vma=False,
    )
```

```python
import jax
import jax.numpy as jnp
from jax import lax
from jax.experimental import pallas as pl
from jax.experimental.pallas import tpu as pltpu
from jax.sharding import PartitionSpec as P

BLK = 128
RB = 8
CB = 4
KP = 4
SIDE = 4
META = 16
HALF = 8
DATA = HALF * BLK
ROWS = DATA + META
MOST = 64
PICKS = 8
NEAR = 16
LISTS = 80
STEP = 8
BUCKETS = 32
ITEMS = 2
NONE = 128
DELTA = (0, SIDE - 1, 1, 2)
STEPS = (1, -1, 2)


def move_a(value, distance, phase):
    pairs = []
    for x in range(SIDE):
        for y in range(SIDE):
            for core in range(2):
                along_y = (core == 0) == (phase == 0)
                tx = x if along_y else (x + distance) % SIDE
                ty = (y + distance) % SIDE if along_y else y
                pairs.append(((x * SIDE + y) * 2 + core, (tx * SIDE + ty) * 2 + core))
    return lax.ppermute(value, ("row", "layer"), pairs)


def move_b(value, distance, depth):
    pairs = []
    for z in range(depth):
        pairs.append((z * 2, ((z + distance) % depth) * 2))
        pairs.append((z * 2 + 1, ((z - distance) % depth) * 2 + 1))
    return lax.ppermute(value, ("col", "layer"), pairs)


def swap(value):
    return lax.ppermute(value, "layer", [(0, 1), (1, 0)])


def pack(
    a_rows, a_cols, b_rows, b_cols, a_blocks, b_blocks, a_out, b_out, ar, ac, br, bc, sem, num_sem
):
    core = lax.axis_index("layer")
    numbers = [
        pltpu.make_async_copy(source, held, num_sem.at[n])
        for n, (source, held) in enumerate(
            ((a_rows, ar), (a_cols, ac), (b_rows, br), (b_cols, bc))
        )
    ]
    for copy in numbers:
        copy.start()
    copies = []
    for i in range(2):
        for t in range(HALF):
            copies.append(
                pltpu.make_async_copy(
                    b_blocks.at[i, 0, t], b_out.at[i, pl.ds(t * BLK, BLK)], sem.at[8 * i + t]
                )
            )
    for s in range(HALF):
        copies.append(
            pltpu.make_async_copy(
                a_blocks.at[0, 0, 2 * s + core], a_out.at[pl.ds(s * BLK, BLK)], sem.at[16 + s]
            )
        )
    for copy in copies:
        copy.start()
    for copy in numbers:
        copy.wait()
    line = lax.broadcasted_iota(jnp.int32, (META, BLK), 0)
    tile = jnp.zeros((META, BLK), jnp.int32)
    for s in range(HALF):
        tile = jnp.where(line == s, ar[0, 0, 2 * s + core], tile)
        tile = jnp.where(line == HALF + s, ac[0, 0, 2 * s + core] * CB, tile)
    a_out[DATA:ROWS, :] = tile.astype(jnp.float32).astype(jnp.bfloat16)
    for i in range(2):
        tile = jnp.zeros((META, BLK), jnp.int32)
        for t in range(HALF):
            tile = jnp.where(line == t, br[i, 0, t] * CB + bc[i, 0, t], tile)
        b_out[i, DATA:ROWS, :] = tile.astype(jnp.float32).astype(jnp.bfloat16)
    for copy in copies:
        copy.wait()


def packed(a_blocks, a_rows, a_cols, b_blocks, b_rows, b_cols):
    vmem = pl.BlockSpec(memory_space=pltpu.VMEM)
    anywhere = pl.BlockSpec(memory_space=pl.ANY)
    return pl.pallas_call(
        pack,
        out_shape=(
            jax.ShapeDtypeStruct((ROWS, BLK), jnp.bfloat16),
            jax.ShapeDtypeStruct((2, ROWS, BLK), jnp.bfloat16),
        ),
        in_specs=[anywhere] * 6,
        out_specs=(vmem,) * 2,
        scratch_shapes=[
            pltpu.SMEM((1, 1, 16), jnp.int32),
            pltpu.SMEM((1, 1, 16), jnp.int32),
            pltpu.SMEM((2, 1, HALF), jnp.int32),
            pltpu.SMEM((2, 1, HALF), jnp.int32),
            pltpu.SemaphoreType.DMA((24,)),
            pltpu.SemaphoreType.DMA((4,)),
        ],
        compiler_params=pltpu.CompilerParams(vmem_limit_bytes=4 * 1024 * 1024),
        name="pack",
    )(
        *[
            pltpu.with_memory_space_constraint(part, pltpu.HBM)
            for part in (a_rows, a_cols, b_rows, b_cols, a_blocks, b_blocks)
        ]
    )


def mark(*refs):
    refs[-1][...] = jnp.zeros_like(refs[-1])


def marker(parts, microseconds):
    return pl.pallas_call(
        mark,
        out_shape=jax.ShapeDtypeStruct((8, BLK), jnp.float32),
        in_specs=[pl.BlockSpec(memory_space=pl.ANY)] * len(parts),
        out_specs=pl.BlockSpec(memory_space=pltpu.VMEM),
        cost_estimate=pl.CostEstimate(
            flops=int(microseconds * 1.15e9), bytes_accessed=0, transcendentals=0
        ),
        compiler_params=pltpu.CompilerParams(vmem_limit_bytes=4 * 1024 * 1024),
        name="marker",
    )(*parts)


def multiply(keep, marked, *refs):
    a_refs, b_refs = refs[:4], refs[4:13]
    send, own, av, bv, am, bm, acc, keys, list_v, lists, flat = refs[13:24]
    data_sem, meta_sem, list_sem, out_sem = refs[24:]
    row, z, core = lax.axis_index("row"), lax.axis_index("col"), lax.axis_index("layer")
    x, y = row // SIDE, row % SIDE
    spots = [(b_refs[0], 0, 2)]
    for t in range(1, 4):
        spots.append((b_refs[t], 2 * jnp.where(core == 0, 8 - t, t), 2))
        spots.append((b_refs[3 + t], 2 * jnp.where(core == 0, t, 8 - t), 2))
    spots.append((b_refs[7], 8 + core, 1))
    spots.append((b_refs[8], 9 - core, 1))
    copies, metas = [], []
    for held, meta, group in (
        (av, am, [(a_refs[g], 4 * g, 4) for g in range(4)]),
        (bv, bm, spots),
    ):
        for ref, at, count in group:
            n = len(copies)
            copies.append(
                pltpu.make_async_copy(
                    ref.at[:, pl.ds(0, DATA), :], held.at[pl.ds(at, count)], data_sem.at[n]
                )
            )
            metas.append(
                pltpu.make_async_copy(
                    ref.at[:, pl.ds(DATA, META), :], meta.at[pl.ds(at, count)], meta_sem.at[n]
                )
            )
    for copy in metas:
        copy.start()
    for copy in copies:
        copy.start()
    av[16, 0:BLK, :] = jnp.zeros((BLK, BLK), jnp.bfloat16)
    none = float(NONE * 128)
    lane = lax.broadcasted_iota(jnp.int32, (HALF, BLK), 1)
    slot = lax.broadcasted_iota(jnp.int32, (HALF, BLK), 0).astype(jnp.float32)
    bucket_row = (lane // CB).astype(jnp.float32)
    bucket_col = (lane % CB).astype(jnp.float32)
    for copy in metas:
        copy.wait()
    count = jnp.zeros((HALF, BLK), jnp.float32)
    for p in range(16):
        first, second = DELTA[p // 4], DELTA[p % 4]
        px = (x + jnp.where(core == 0, first, second)) % SIDE
        py = (y + jnp.where(core == 0, second, first)) % SIDE
        k = (px * SIDE + py + 2 * z) % 16
        q = (k - row + 16) % 16
        spot = ((q // 2 - z + 8) % 8) * 2 + q % 2
        numbers = am[p].astype(jnp.float32)
        wanted = numbers[HALF:, :] + bucket_col
        b_numbers = bm[spot].astype(jnp.float32)
        found = jnp.zeros((HALF, BLK), jnp.float32)
        for t in range(HALF):
            found = jnp.where(b_numbers[t : t + 1, :] == wanted, t + 1.0, found)
        kept = keep[pl.ds(k, 1), :].astype(jnp.float32)
        valid = jnp.where(numbers[:HALF, :] == bucket_row, kept, 0.0)
        valid = (valid != 0.0) & (found != 0.0)
        base = (p * HALF * 128 - 1 + spot * HALF).astype(jnp.float32)
        keys[p] = jnp.where(valid, base + slot * 128.0 + found, none)
        count = count + jnp.where(valid, 1.0, 0.0)
    count = jnp.sum(count, axis=0, keepdims=True)
    list_v[0:1, :] = count.astype(jnp.int32)
    largest = jnp.max(count).astype(jnp.int32)

    def pick(j):
        least = keys[0]
        for p in range(1, 16):
            least = jnp.minimum(least, keys[p])
        least = jnp.min(least, axis=0, keepdims=True)
        list_v[pl.ds(1 + j, 1), :] = least.astype(jnp.int32)
        for p in range(16):
            keys[p] = jnp.where(keys[p] == least, none, keys[p])

    for j in range(PICKS):
        pick(j)
    first_part = pltpu.make_async_copy(
        list_v.at[pl.ds(0, NEAR)], lists.at[pl.ds(0, NEAR)], list_sem.at[0]
    )
    first_part.start()
    first_part.wait()

    @pl.when(largest > PICKS)
    def _():
        def more(j, carry):
            pick(j)
            return carry

        lax.fori_loop(PICKS, largest, more, 0)
        whole = pltpu.make_async_copy(list_v, lists, list_sem.at[1])
        whole.start()
        whole.wait()

    def bucket(b, n):
        length = lists[0, b]
        for j in range(2):
            flat[n + j] = lists[1 + ITEMS + j, b] * BUCKETS + b

        def item(j, carry):
            flat[n + j - ITEMS] = lists[1 + j, b] * BUCKETS + b
            return carry

        lax.fori_loop(ITEMS + 2, jnp.maximum(length, ITEMS + 2), item, 0)
        return n + jnp.maximum(length - ITEMS, 0)

    total = lax.fori_loop(0, BUCKETS, bucket, 0, unroll=4)
    for j in range(STEP):
        flat[total + j] = NONE * 128 * BUCKETS
    for copy in copies:
        copy.wait()

    def blocks_of(code):
        ia, ib = code // 128, code % 128
        return (
            av[ia // HALF, pl.ds(pl.multiple_of((ia % HALF) * BLK, BLK), BLK), :],
            bv[ib // HALF, pl.ds(pl.multiple_of((ib % HALF) * BLK, BLK), BLK), :],
        )

    for b in range(BUCKETS):
        pairs = [blocks_of(lists[1 + j, b]) for j in range(ITEMS)]
        acc[b] = jnp.dot(
            jnp.concatenate([left for left, _ in pairs], axis=1),
            jnp.concatenate([right for _, right in pairs], axis=0),
            preferred_element_type=jnp.float32,
        )

    def step(i, carry):
        for j in range(STEP):
            code = flat[i * STEP + j]
            left, right = blocks_of(code // BUCKETS)
            acc[code % BUCKETS] += jnp.dot(left, right, preferred_element_type=jnp.float32)
        return carry

    lax.fori_loop(0, (total + STEP - 1) // STEP, step, 0)
    keeping = []
    for n, (out, base) in enumerate(((send, 2 * (1 - core)), (own, 2 * core))):
        for r in range(RB):
            keeping.append(
                pltpu.make_async_copy(
                    acc.at[pl.ds(r * CB + base, 2)], out.at[pl.ds(2 * r, 2)], out_sem.at[n, r]
                )
            )
    for copy in keeping:
        copy.start()
    for copy in keeping:
        copy.wait()


def partial_sums(keep, a_parts, b_parts):
    vmem = pl.BlockSpec(memory_space=pltpu.VMEM)
    anywhere = pl.BlockSpec(memory_space=pl.ANY)
    half = jax.ShapeDtypeStruct((2 * RB, BLK, BLK), jnp.float32)
    return pl.pallas_call(
        multiply,
        out_shape=(half, pltpu.HBM(half.shape, half.dtype)),
        in_specs=[vmem, vmem] + [anywhere] * 13,
        out_specs=(anywhere, anywhere),
        scratch_shapes=[
            pltpu.VMEM((17, DATA, BLK), jnp.bfloat16),
            pltpu.VMEM((16, DATA, BLK), jnp.bfloat16),
            pltpu.VMEM((16, META, BLK), jnp.bfloat16),
            pltpu.VMEM((16, META, BLK), jnp.bfloat16),
            pltpu.VMEM((BUCKETS, BLK, BLK), jnp.float32),
            pltpu.VMEM((16, HALF, BLK), jnp.float32),
            pltpu.VMEM((LISTS, BLK), jnp.int32),
            pltpu.SMEM((LISTS, BLK), jnp.int32),
            pltpu.SMEM((BUCKETS * MOST + 2 * STEP,), jnp.int32),
            pltpu.SemaphoreType.DMA((13,)),
            pltpu.SemaphoreType.DMA((13,)),
            pltpu.SemaphoreType.DMA((2,)),
            pltpu.SemaphoreType.DMA((2, RB)),
        ],
        compiler_params=pltpu.CompilerParams(vmem_limit_bytes=28 * 1024 * 1024),
        name="multiply",
    )(keep, marker(a_parts[1:], 10), *a_parts, *b_parts)


def finish(keep_in, own, other, out, held, made, keep, sem, out_sem, keep_sem):
    keeps = pltpu.make_async_copy(keep_in, keep, keep_sem)
    keeps.start()
    copies = [
        pltpu.make_async_copy(
            source.at[pl.ds(4 * r, 4)], held.at[i, pl.ds(4 * r, 4)], sem.at[i, r]
        )
        for r in range(RB // 2)
        for i, source in enumerate((own, other))
    ]
    for copy in copies:
        copy.start()
    keeps.wait()
    written = []
    for r in range(RB // 2):
        copies[2 * r].wait()
        copies[2 * r + 1].wait()
        for b in range(4 * r, 4 * r + 4):
            total = (held[0, b] + held[1, b]) * keep[b // 2, b % 2].astype(jnp.float32)
            cols = slice(b % 2 * BLK, (b % 2 + 1) * BLK)
            made[b // 2 * BLK : (b // 2 + 1) * BLK, cols] = total.astype(jnp.bfloat16)
        rows = pl.ds(2 * r * BLK, 2 * BLK)
        written.append(pltpu.make_async_copy(made.at[rows], out.at[rows], out_sem.at[r]))
        written[-1].start()
    for copy in written:
        copy.wait()


def filtered(keep, own, other):
    anywhere = pl.BlockSpec(memory_space=pl.ANY)
    return pl.pallas_call(
        finish,
        out_shape=jax.ShapeDtypeStruct((RB * BLK, 2 * BLK), jnp.bfloat16),
        in_specs=[anywhere] * 3,
        out_specs=anywhere,
        scratch_shapes=[
            pltpu.VMEM((2, 2 * RB, BLK, BLK), jnp.float32),
            pltpu.VMEM((RB * BLK, 2 * BLK), jnp.bfloat16),
            pltpu.SMEM((RB, 2), jnp.int32),
            pltpu.SemaphoreType.DMA((2, RB // 2)),
            pltpu.SemaphoreType.DMA((RB // 2,)),
            pltpu.SemaphoreType.DMA,
        ],
        compiler_params=pltpu.CompilerParams(vmem_limit_bytes=8 * 1024 * 1024),
        name="finish",
    )(keep, pltpu.with_memory_space_constraint(own, pltpu.HBM), other)


def body(a_blocks, a_rows, a_cols, b_blocks, b_rows, b_cols, prod_keep, res_keep):
    depth = lax.axis_size("col")
    core = lax.axis_index("layer")
    keep = prod_keep.transpose(1, 0, 2).reshape(16, RB * CB)
    keep = jnp.pad(keep, ((0, 0), (0, BLK - RB * CB)))

    a_mine, b_mine = packed(a_blocks, a_rows, a_cols, b_blocks, b_rows, b_cols)

    b_one = move_b(b_mine, 1, depth)
    b_two, b_one_back = lax.optimization_barrier((move_b(b_one, 1, depth), swap(b_one)))
    b_three = move_b(b_two, 1, depth)
    part = jnp.where(core == 0, b_two[:1], b_two[1:])
    part, b_two_back = lax.optimization_barrier((part, swap(b_two)))
    last = move_b(part, 2, depth)
    b_from = [b_mine, b_one, b_two, b_three]
    b_theirs = [b_one_back, b_two_back, swap(b_three)]

    a_own = jnp.stack([a_mine] + [move_a(a_mine, d, 0) for d in STEPS])
    a_parts = [a_own] + [move_a(a_own, d, 1) for d in STEPS]

    send, own = partial_sums(keep, a_parts, b_from + b_theirs + [last, swap(last)])
    return filtered(res_keep, own, swap(send))


def solution(mesh):
    return jax.shard_map(
        body,
        mesh=mesh,
        in_specs=(
            P("col", "row", None, None, None),
            P("col", "row", None),
            P("col", "row", None),
            P("col", "row", None, None, None),
            P("col", "row", None),
            P("col", "row", None),
            P("col", None, "row"),
            P("col", ("row", "layer")),
        ),
        out_specs=P("col", ("row", "layer")),
        check_vma=False,
    )
```

```python
import jax
import jax.numpy as jnp
from jax import lax
from jax.experimental import pallas as pl
from jax.experimental.pallas import tpu as pltpu
from jax.sharding import PartitionSpec as P

BLK = 128
RB = 8
CB = 4
KP = 4
SIDE = 4
META = 16
HALF = 8
DATA = HALF * BLK
ROWS = DATA + META
MOST = 64
PICKS = 10
NEAR = 16
LISTS = 80
STEP = 16
BUCKETS = 32
ITEMS = 2
NONE = 128
DELTA = (0, 2, SIDE - 1, 1)
STEPS = (2, 1, -1)


def move_a(value, distance, phase):
    pairs = []
    for x in range(SIDE):
        for y in range(SIDE):
            for core in range(2):
                along_y = (core == 0) == (phase == 0)
                tx = x if along_y else (x + distance) % SIDE
                ty = (y + distance) % SIDE if along_y else y
                pairs.append(((x * SIDE + y) * 2 + core, (tx * SIDE + ty) * 2 + core))
    return lax.ppermute(value, ("row", "layer"), pairs)


def move_b(value, distance, depth):
    pairs = []
    for z in range(depth):
        pairs.append((z * 2, ((z + distance) % depth) * 2))
        pairs.append((z * 2 + 1, ((z - distance) % depth) * 2 + 1))
    return lax.ppermute(value, ("col", "layer"), pairs)


def swap(value):
    return lax.ppermute(value, "layer", [(0, 1), (1, 0)])


def pack(
    a_rows, a_cols, b_rows, b_cols, a_blocks, b_blocks, a_out, b_out, ar, ac, br, bc, sem, num_sem
):
    core = lax.axis_index("layer")
    numbers = [
        pltpu.make_async_copy(source, held, num_sem.at[n])
        for n, (source, held) in enumerate(
            ((a_rows, ar), (a_cols, ac), (b_rows, br), (b_cols, bc))
        )
    ]
    for copy in numbers:
        copy.start()
    copies = []
    for i in range(2):
        for t in range(HALF):
            copies.append(
                pltpu.make_async_copy(
                    b_blocks.at[i, 0, t], b_out.at[i, pl.ds(t * BLK, BLK)], sem.at[8 * i + t]
                )
            )
    for s in range(HALF):
        copies.append(
            pltpu.make_async_copy(
                a_blocks.at[0, 0, 2 * s + core], a_out.at[pl.ds(s * BLK, BLK)], sem.at[16 + s]
            )
        )
    for copy in copies:
        copy.start()
    for copy in numbers:
        copy.wait()
    line = lax.broadcasted_iota(jnp.int32, (META, BLK), 0)
    tile = jnp.zeros((META, BLK), jnp.int32)
    for s in range(HALF):
        tile = jnp.where(line == s, ar[0, 0, 2 * s + core], tile)
        tile = jnp.where(line == HALF + s, ac[0, 0, 2 * s + core] * CB, tile)
    a_out[DATA:ROWS, :] = tile.astype(jnp.float32).astype(jnp.bfloat16)
    for i in range(2):
        tile = jnp.zeros((META, BLK), jnp.int32)
        for t in range(HALF):
            tile = jnp.where(line == t, br[i, 0, t] * CB + bc[i, 0, t], tile)
        b_out[i, DATA:ROWS, :] = tile.astype(jnp.float32).astype(jnp.bfloat16)
    for copy in copies:
        copy.wait()


def packed(a_blocks, a_rows, a_cols, b_blocks, b_rows, b_cols):
    vmem = pl.BlockSpec(memory_space=pltpu.VMEM)
    anywhere = pl.BlockSpec(memory_space=pl.ANY)
    return pl.pallas_call(
        pack,
        out_shape=(
            jax.ShapeDtypeStruct((ROWS, BLK), jnp.bfloat16),
            jax.ShapeDtypeStruct((2, ROWS, BLK), jnp.bfloat16),
        ),
        in_specs=[anywhere] * 6,
        out_specs=(vmem,) * 2,
        scratch_shapes=[
            pltpu.SMEM((1, 1, 16), jnp.int32),
            pltpu.SMEM((1, 1, 16), jnp.int32),
            pltpu.SMEM((2, 1, HALF), jnp.int32),
            pltpu.SMEM((2, 1, HALF), jnp.int32),
            pltpu.SemaphoreType.DMA((24,)),
            pltpu.SemaphoreType.DMA((4,)),
        ],
        compiler_params=pltpu.CompilerParams(vmem_limit_bytes=4 * 1024 * 1024),
        name="pack",
    )(
        *[
            pltpu.with_memory_space_constraint(part, pltpu.HBM)
            for part in (a_rows, a_cols, b_rows, b_cols, a_blocks, b_blocks)
        ]
    )


def mark(*refs):
    refs[-1][...] = jnp.zeros_like(refs[-1])


def marker(parts, microseconds):
    return pl.pallas_call(
        mark,
        out_shape=jax.ShapeDtypeStruct((8, BLK), jnp.float32),
        in_specs=[pl.BlockSpec(memory_space=pl.ANY)] * len(parts),
        out_specs=pl.BlockSpec(memory_space=pltpu.VMEM),
        cost_estimate=pl.CostEstimate(
            flops=int(microseconds * 1.15e9), bytes_accessed=0, transcendentals=0
        ),
        compiler_params=pltpu.CompilerParams(vmem_limit_bytes=4 * 1024 * 1024),
        name="marker",
    )(*parts)


def multiply(keep, marked, *refs):
    a_refs, b_refs = refs[:4], refs[4:13]
    send, own, av, bv, am, bm, acc, keys, list_v, lists, flat = refs[13:24]
    data_sem, meta_sem, list_sem, out_sem = refs[24:]
    row, z, core = lax.axis_index("row"), lax.axis_index("col"), lax.axis_index("layer")
    x, y = row // SIDE, row % SIDE
    spots = [(b_refs[0], 0, 2)]
    for t in range(1, 4):
        spots.append((b_refs[t], 2 * jnp.where(core == 0, 8 - t, t), 2))
        spots.append((b_refs[3 + t], 2 * jnp.where(core == 0, t, 8 - t), 2))
    spots.append((b_refs[7], 8 + core, 1))
    spots.append((b_refs[8], 9 - core, 1))
    copies, metas = [], []
    for held, meta, group in (
        (av, am, [(a_refs[g], 4 * g, 4) for g in range(4)]),
        (bv, bm, spots),
    ):
        for ref, at, count in group:
            n = len(copies)
            copies.append(
                pltpu.make_async_copy(
                    ref.at[:, pl.ds(0, DATA), :], held.at[pl.ds(at, count)], data_sem.at[n]
                )
            )
            metas.append(
                pltpu.make_async_copy(
                    ref.at[:, pl.ds(DATA, META), :], meta.at[pl.ds(at, count)], meta_sem.at[n]
                )
            )
    for copy in metas:
        copy.start()
    for copy in copies:
        copy.start()
    av[16, 0:BLK, :] = jnp.zeros((BLK, BLK), jnp.bfloat16)
    none = float(NONE * 128)
    lane = lax.broadcasted_iota(jnp.int32, (HALF, BLK), 1)
    slot = lax.broadcasted_iota(jnp.int32, (HALF, BLK), 0).astype(jnp.float32)
    bucket_row = (lane // CB).astype(jnp.float32)
    bucket_col = (lane % CB).astype(jnp.float32)
    for copy in metas:
        copy.wait()
    count = jnp.zeros((HALF, BLK), jnp.float32)
    for p in range(16):
        first, second = DELTA[p // 4], DELTA[p % 4]
        px = (x + jnp.where(core == 0, first, second)) % SIDE
        py = (y + jnp.where(core == 0, second, first)) % SIDE
        k = (px * SIDE + py + 2 * z) % 16
        q = (k - row + 16) % 16
        spot = ((q // 2 - z + 8) % 8) * 2 + q % 2
        numbers = am[p].astype(jnp.float32)
        wanted = numbers[HALF:, :] + bucket_col
        b_numbers = bm[spot].astype(jnp.float32)
        found = jnp.zeros((HALF, BLK), jnp.float32)
        for t in range(HALF):
            found = jnp.where(b_numbers[t : t + 1, :] == wanted, t + 1.0, found)
        kept = keep[pl.ds(k, 1), :].astype(jnp.float32)
        valid = jnp.where(numbers[:HALF, :] == bucket_row, kept, 0.0)
        valid = (valid != 0.0) & (found != 0.0)
        base = (p * HALF * 128 - 1 + spot * HALF).astype(jnp.float32)
        keys[p] = jnp.where(valid, base + slot * 128.0 + found, none)
        count = count + jnp.where(valid, 1.0, 0.0)
    count = jnp.sum(count, axis=0, keepdims=True)
    most = jnp.max(count, axis=1, keepdims=True)
    last_lane = lax.broadcasted_iota(jnp.int32, (1, BLK), 1) == BLK - 1
    list_v[0:1, :] = jnp.where(last_lane, most, count).astype(jnp.int32)

    def pick(j):
        least = keys[0]
        for p in range(1, 16):
            least = jnp.minimum(least, keys[p])
        least = jnp.min(least, axis=0, keepdims=True)
        list_v[pl.ds(1 + j, 1), :] = least.astype(jnp.int32)
        for p in range(16):
            keys[p] = jnp.where(keys[p] == least, none, keys[p])

    for j in range(PICKS):
        pick(j)
    first_part = pltpu.make_async_copy(
        list_v.at[pl.ds(0, NEAR)], lists.at[pl.ds(0, NEAR)], list_sem.at[0]
    )
    first_part.start()
    first_part.wait()
    largest = lists[0, BLK - 1]

    @pl.when(largest > PICKS)
    def _():
        def more(j, carry):
            pick(j)
            return carry

        lax.fori_loop(PICKS, largest, more, 0)
        whole = pltpu.make_async_copy(list_v, lists, list_sem.at[1])
        whole.start()
        whole.wait()

    def bucket(b, n):
        length = lists[0, b]
        for j in range(2):
            flat[n + j] = lists[1 + ITEMS + j, b] * BUCKETS + b

        def item(j, carry):
            flat[n + j - ITEMS] = lists[1 + j, b] * BUCKETS + b
            return carry

        lax.fori_loop(ITEMS + 2, jnp.maximum(length, ITEMS + 2), item, 0)
        return n + jnp.maximum(length - ITEMS, 0)

    total = lax.fori_loop(0, BUCKETS, bucket, 0, unroll=4)
    for j in range(STEP):
        flat[total + j] = NONE * 128 * BUCKETS
    for copy in copies:
        copy.wait()

    def blocks_of(code):
        ia, ib = code // 128, code % 128
        return (
            av[ia // HALF, pl.ds(pl.multiple_of((ia % HALF) * BLK, BLK), BLK), :],
            bv[ib // HALF, pl.ds(pl.multiple_of((ib % HALF) * BLK, BLK), BLK), :],
        )

    for b in range(BUCKETS):
        pairs = [blocks_of(lists[1 + j, b]) for j in range(ITEMS)]
        acc[b // CB, b % CB] = jnp.dot(
            jnp.concatenate([left for left, _ in pairs], axis=1),
            jnp.concatenate([right for _, right in pairs], axis=0),
            preferred_element_type=jnp.float32,
        )

    def step(i, carry):
        for j in range(STEP):
            code = flat[i * STEP + j]
            left, right = blocks_of(code // BUCKETS)
            b = code % BUCKETS
            acc[b // CB, b % CB] += jnp.dot(left, right, preferred_element_type=jnp.float32)
        return carry

    lax.fori_loop(0, (total + STEP - 1) // STEP, step, 0)
    keeping = [
        pltpu.make_async_copy(acc.at[:, pl.ds(base, 2)], out, out_sem.at[n])
        for n, (out, base) in enumerate(((send, 2 * (1 - core)), (own, 2 * core)))
    ]
    for copy in keeping:
        copy.start()
    for copy in keeping:
        copy.wait()


def partial_sums(keep, a_parts, b_parts):
    vmem = pl.BlockSpec(memory_space=pltpu.VMEM)
    anywhere = pl.BlockSpec(memory_space=pl.ANY)
    half = jax.ShapeDtypeStruct((RB, 2, BLK, BLK), jnp.float32)
    return pl.pallas_call(
        multiply,
        out_shape=(half, pltpu.HBM(half.shape, half.dtype)),
        in_specs=[vmem, vmem] + [anywhere] * 13,
        out_specs=(anywhere, anywhere),
        scratch_shapes=[
            pltpu.VMEM((17, DATA, BLK), jnp.bfloat16),
            pltpu.VMEM((16, DATA, BLK), jnp.bfloat16),
            pltpu.VMEM((16, META, BLK), jnp.bfloat16),
            pltpu.VMEM((16, META, BLK), jnp.bfloat16),
            pltpu.VMEM((RB, CB, BLK, BLK), jnp.float32),
            pltpu.VMEM((16, HALF, BLK), jnp.float32),
            pltpu.VMEM((LISTS, BLK), jnp.int32),
            pltpu.SMEM((LISTS, BLK), jnp.int32),
            pltpu.SMEM((BUCKETS * MOST + 2 * STEP,), jnp.int32),
            pltpu.SemaphoreType.DMA((13,)),
            pltpu.SemaphoreType.DMA((13,)),
            pltpu.SemaphoreType.DMA((2,)),
            pltpu.SemaphoreType.DMA((2,)),
        ],
        compiler_params=pltpu.CompilerParams(vmem_limit_bytes=28 * 1024 * 1024),
        name="multiply",
    )(keep, marker(a_parts[1:], 10), *a_parts, *b_parts)


def finish(keep_in, own, other, out, held, made, keep, sem, out_sem, keep_sem):
    keeps = pltpu.make_async_copy(keep_in, keep, keep_sem)
    keeps.start()
    copies = [
        pltpu.make_async_copy(
            source.at[pl.ds(2 * r, 2)], held.at[i, pl.ds(2 * r, 2)], sem.at[i, r]
        )
        for r in range(RB // 2)
        for i, source in enumerate((own, other))
    ]
    for copy in copies:
        copy.start()
    keeps.wait()
    written = []
    for r in range(RB // 2):
        copies[2 * r].wait()
        copies[2 * r + 1].wait()
        for b in range(4 * r, 4 * r + 4):
            at = (b // 2, b % 2)
            total = (held[0, *at] + held[1, *at]) * keep[at].astype(jnp.float32)
            cols = slice(b % 2 * BLK, (b % 2 + 1) * BLK)
            made[b // 2 * BLK : (b // 2 + 1) * BLK, cols] = total.astype(jnp.bfloat16)
        rows = pl.ds(2 * r * BLK, 2 * BLK)
        written.append(pltpu.make_async_copy(made.at[rows], out.at[rows], out_sem.at[r]))
        written[-1].start()
    for copy in written:
        copy.wait()


def filtered(keep, own, other):
    anywhere = pl.BlockSpec(memory_space=pl.ANY)
    return pl.pallas_call(
        finish,
        out_shape=jax.ShapeDtypeStruct((RB * BLK, 2 * BLK), jnp.bfloat16),
        in_specs=[anywhere] * 3,
        out_specs=anywhere,
        scratch_shapes=[
            pltpu.VMEM((2, RB, 2, BLK, BLK), jnp.float32),
            pltpu.VMEM((RB * BLK, 2 * BLK), jnp.bfloat16),
            pltpu.SMEM((RB, 2), jnp.int32),
            pltpu.SemaphoreType.DMA((2, RB // 2)),
            pltpu.SemaphoreType.DMA((RB // 2,)),
            pltpu.SemaphoreType.DMA,
        ],
        compiler_params=pltpu.CompilerParams(vmem_limit_bytes=8 * 1024 * 1024),
        name="finish",
    )(keep, pltpu.with_memory_space_constraint(own, pltpu.HBM), other)


def body(a_blocks, a_rows, a_cols, b_blocks, b_rows, b_cols, prod_keep, res_keep):
    depth = lax.axis_size("col")
    core = lax.axis_index("layer")
    keep = prod_keep.transpose(1, 0, 2).reshape(16, RB * CB)
    keep = jnp.pad(keep, ((0, 0), (0, BLK - RB * CB)))

    a_mine, b_mine = packed(a_blocks, a_rows, a_cols, b_blocks, b_rows, b_cols)

    b_one = move_b(b_mine, 1, depth)
    b_two, b_one_back = lax.optimization_barrier((move_b(b_one, 1, depth), swap(b_one)))
    b_three = move_b(b_two, 1, depth)
    part = jnp.where(core == 0, b_two[:1], b_two[1:])
    part, b_two_back = lax.optimization_barrier((part, swap(b_two)))
    last = move_b(part, 2, depth)
    b_from = [b_mine, b_one, b_two, b_three]
    b_theirs = [b_one_back, b_two_back, swap(b_three)]

    a_own = jnp.stack([a_mine] + [move_a(a_mine, d, 0) for d in STEPS])
    a_parts = [a_own] + [move_a(a_own, d, 1) for d in STEPS]

    send, own = partial_sums(keep, a_parts, b_from + b_theirs + [last, swap(last)])
    return filtered(res_keep, own, swap(send))


def solution(mesh):
    return jax.shard_map(
        body,
        mesh=mesh,
        in_specs=(
            P("col", "row", None, None, None),
            P("col", "row", None),
            P("col", "row", None),
            P("col", "row", None, None, None),
            P("col", "row", None),
            P("col", "row", None),
            P("col", None, "row"),
            P("col", ("row", "layer")),
        ),
        out_specs=P("col", ("row", "layer")),
        check_vma=False,
    )
```
